32 devices in a mesh: ens: 2 (over y), tm: 4 (over z), space: 4 (over x, core).
Axes of the slice: x: 2, y: 2, z: 4, core: 2. Of those that a mesh axis runs over, the one named last changes fastest.
Arguments:
- initial: float32 [512, 2048], P(('ens', 'space')), parts along dimension 0, may hold values from -6 to 6
- diffusivity: float32 [512, 2048], P(('ens', 'space')), parts along dimension 0, may hold values from 0.04 to 0.06
- velocity_x: float32 [512, 2048], P(('ens', 'space')), parts along dimension 0, may hold values from -0.08 to 0.08
- velocity_y: float32 [512, 2048], P(('ens', 'space')), parts along dimension 0, may hold values from -0.08 to 0.08
- source: float32 [512, 2048], P(('ens', 'space')), parts along dimension 0, may hold values from -0.3 to 0.3
Outputs:
- end_states: float32 [4, 512, 2048], P('tm', ('ens', 'space')), parts along dimension 1
The draws below stay inside these ranges and needn't reach their ends.
There are 2 independent parts, one for each index of `ens`. The reference program is written for one: setup_inputs(seed, part) draws one part's arguments, and reference() takes and returns one part's arrays. A program takes and returns all parts, laid end to end along the dimension named above; each array names one. Nothing has to cross between parts.
All inputs are finite; a program needn't handle non-finite values.
Results may differ from the reference program's by a relative error of at most 0.0045.
Values may be sent and summed in bfloat16 or wider, within the bound.
A program may use at most 64 MiB of HBM per device.

```python
import math
import jax
import jax.numpy as jnp
from jax import lax

COLS = 2048
FINE = 4
NR = 256
SLICES = 4


def shard_levels(stream_key, dims, split, least, largest):
    level, own = 1.0, jax.random.fold_in(stream_key, 6)
    for dim, parts in split:
        steps = jnp.exp(jax.random.uniform(jax.random.fold_in(own, dim), (parts,), jnp.float32, least / len(split), largest / len(split)))
        level = level * jnp.repeat(steps, dims[dim] // parts).reshape([-1 if axis == dim else 1 for axis in range(len(dims))])
    return level


def bell_draw(stream_key, dims, width, limit, shards=(), dtype=jnp.bfloat16):
    array = width * jax.random.normal(stream_key, dims, jnp.float32)
    if shards:
        array = array * shard_levels(stream_key, dims, shards, -0.22, 0.18)
    return jnp.clip(array, -limit, limit).astype(dtype)


def setup_inputs(seed: int = 0, part: int = 0) -> dict:
    key_of = jax.random.split(jax.random.key(seed), 6)
    part_splits = jax.random.split(jax.random.fold_in(key_of[5], part), 6)
    initial = bell_draw(part_splits[0], (NR, COLS), 1.0, 6.0, ((0, 4),), jnp.float32)
    diffusivity = jnp.clip(jnp.exp(math.log(0.06) - 0.4054651 * jax.random.uniform(part_splits[1], (NR, COLS), jnp.float32) ** shard_levels(part_splits[1], (NR, COLS), ((0, 4),), -0.2, 0.2)), 0.04, 0.06)
    velocity_x = jnp.clip(jax.random.uniform(part_splits[2], (NR, COLS), jnp.float32, -0.08, 0.08) * shard_levels(part_splits[2], (NR, COLS), ((0, 4),), -0.4, 0.0), -0.08, 0.08)
    velocity_y = jnp.clip(jax.random.uniform(part_splits[3], (NR, COLS), jnp.float32, -0.08, 0.08) * shard_levels(part_splits[3], (NR, COLS), ((0, 4),), -0.4, 0.0), -0.08, 0.08)
    source = bell_draw(part_splits[4], (NR, COLS), 0.05, 0.3, ((0, 4),), jnp.float32)
    return {"initial": initial, "diffusivity": diffusivity, "velocity_x": velocity_x, "velocity_y": velocity_y, "source": source}


def tendency(padded, diffusivity, velocity_x, velocity_y):
    centre = padded[1:-1]
    north_row = padded[:-2]
    south_row = padded[2:]
    east_col = jnp.roll(centre, -1, axis=1)
    west_col = jnp.roll(centre, 1, axis=1)
    lapl = east_col + west_col + north_row + south_row - 4.0 * centre
    return diffusivity * lapl - 0.5 * (velocity_x * (east_col - west_col) + velocity_y * (south_row - north_row))


def fine_step(padded, diffusivity, velocity_x, velocity_y, source):
    return padded[1:-1] + tendency(padded, diffusivity, velocity_x, velocity_y) + source


def coarse_step(padded, coef_set):
    values = padded.astype(jnp.float32)
    diff_c = coef_set[0].astype(jnp.float32)
    vel_xc = coef_set[1].astype(jnp.float32)
    vel_yc = coef_set[2].astype(jnp.float32)
    source_c = coef_set[3].astype(jnp.float32)
    return values[1:-1] + 4.0 * tendency(values, diff_c, vel_xc, vel_yc) + 4.0 * source_c


def reference(initial, diffusivity, velocity_x, velocity_y, source):
    coarse_set = tuple(c.astype(jnp.bfloat16) for c in (diffusivity, velocity_x, velocity_y, source))
    initial_c = initial.astype(jnp.bfloat16)

    def fine_prop(state_field):
        for turn_idx in range(FINE):
            padded = jnp.pad(state_field, ((1, 1), (0, 0)))
            state_field = fine_step(padded, diffusivity, velocity_x, velocity_y, source)
        return state_field

    def coarse_whole(state_now):
        return coarse_step(jnp.pad(state_now, ((1, 1), (0, 0))), coarse_set)

    delta_zero = (fine_prop(initial) - coarse_whole(initial_c)).astype(jnp.bfloat16)

    def first_sweep(state_now, unused):
        next_state = (coarse_whole(state_now) + delta_zero.astype(jnp.float32)).astype(jnp.bfloat16)
        return next_state, state_now

    last_one, starts_one = lax.scan(first_sweep, initial_c, None, length=SLICES)

    def correction(state_now):
        return (fine_prop(state_now.astype(jnp.float32)) - coarse_whole(state_now)).astype(jnp.bfloat16)

    deltas_one = lax.map(correction, starts_one)

    def second_sweep(state_now, delta_piece):
        ending = coarse_whole(state_now) + delta_piece.astype(jnp.float32)
        return ending.astype(jnp.bfloat16), ending

    last_two, end_states = lax.scan(second_sweep, initial_c, deltas_one)
    return end_states
```

```python
import functools
from fractions import Fraction

import jax
import jax.numpy as jnp
from jax import lax
from jax.experimental import pallas as pl
from jax.experimental.pallas import tpu as pltpu
from jax.sharding import PartitionSpec as P

FINE = 4
TILE = 8
MESH = pl.DeviceIdType.MESH


def poly_add(a, b, sign=1):
    size = max(len(a), len(b))
    a, b = (list(x) + [Fraction(0)] * (size - len(x)) for x in (a, b))
    return [x + sign * y for x, y in zip(a, b)]


def poly_mul(a, b):
    out = [Fraction(0)] * (len(a) + len(b) - 1)
    for i, x in enumerate(a):
        for j, y in enumerate(b):
            out[i + j] += x * y
    return out


def end_polynomials(slices):
    fine_step = [Fraction(FINE - 1, FINE), Fraction(1, FINE)]
    power, total = [Fraction(1)], [Fraction(0)]
    for _ in range(FINE):
        total = poly_add(total, power)
        power = poly_mul(power, fine_step)

    def fine(q):
        return poly_add(poly_mul(power, q), total)

    def coarse(q):
        return poly_add([Fraction(0)] + list(q), [Fraction(FINE)])

    start_one = start_two = [Fraction(0)]
    delta_zero = poly_add(fine(start_one), coarse(start_one), -1)
    ends = []
    for _ in range(slices):
        delta_one = poly_add(fine(start_one), coarse(start_one), -1)
        start_two = poly_add(coarse(start_two), delta_one)
        ends.append(list(start_two))
        start_one = poly_add(coarse(start_one), delta_zero)
    for q in ends:
        while len(q) > 1 and q[-1] == 0:
            q.pop()
    degree = max(len(q) for q in ends) - 1
    return [[float(c) for c in q] + [0.0] * (degree + 1 - len(q)) for q in ends]


def neighbours(centre, above, below):
    rows, cols = centre.shape
    sub = lax.broadcasted_iota(jnp.int32, (rows, cols), 0)
    east = pltpu.roll(centre, cols - 1, 1)
    west = pltpu.roll(centre, 1, 1)
    north = pltpu.roll(jnp.where(sub == rows - 1, above, centre), 1, 0)
    south = pltpu.roll(jnp.where(sub == 0, below, centre), rows - 1, 0)
    return east, west, north, south


def kernel(table, halo, pad, blocks, *refs):
    args, out_ref = refs[:5], refs[5]
    raw, wts, g_ref, y_ref, send, recv, in_sem, send_sem, recv_sem = refs[6:]
    rows, cols = args[0].shape
    tiles = (rows + 2 * pad) // TILE
    first, last = pad // TILE, (pad + rows) // TILE
    degree = len(table[0]) - 1
    me, turn = lax.axis_index("space"), lax.axis_index("tm")
    has = (me > 0, me < blocks - 1)
    peer = (me - 1, me + 1)

    loads = [
        pltpu.make_async_copy(args[a], raw.at[a, pl.ds(pad, rows)], in_sem.at[a])
        for a in range(5)
    ]
    for load in loads:
        load.start()
    barrier = pltpu.get_barrier_semaphore()
    for side in range(2):
        @pl.when(has[side])
        def _():
            pl.semaphore_signal(
                barrier, inc=1, device_id={"space": peer[side]}, device_id_type=MESH
            )

    def remote(side, slot):
        return pltpu.make_async_remote_copy(
            src_ref=send.at[side],
            dst_ref=recv.at[slot],
            send_sem=send_sem.at[side],
            recv_sem=recv_sem.at[slot],
            device_id={"space": peer[side]},
            device_id_type=MESH,
        )

    for a in range(5):
        loads[a].wait()
        send[0, a] = raw[a, pl.ds(pad, pad), :].astype(jnp.bfloat16)
        send[1, a] = raw[a, pl.ds(rows, pad), :].astype(jnp.bfloat16)
    peers = has[0].astype(jnp.int32) + has[1].astype(jnp.int32)
    pl.semaphore_wait(barrier, peers)
    for side in range(2):
        @pl.when(has[side])
        def _():
            remote(side, 1 - side).start()

    def at(t):
        return pl.ds(pl.multiple_of(t * TILE, TILE), TILE)

    def trio(ref, t):
        return (
            ref[at(t), :],
            ref[at(jnp.maximum(t - 1, 0)), :],
            ref[at(jnp.minimum(t + 1, tiles - 1)), :],
        )

    def apply(centre, around, w):
        east, west, north, south = around
        return (w[0] * east + w[1] * west) + (w[2] * north + w[3] * south) + w[4] * centre

    def prepare(lo, hi):
        def body(t, carry):
            k = 4.0 * raw[1, at(t), :]
            p, r = 2.0 * raw[2, at(t), :], 2.0 * raw[3, at(t), :]
            w = (k - p, k + p, k + r, k - r, 1.0 - 4.0 * k)
            for j in range(5):
                wts[j, at(t), :] = w[j]
            centre, above, below = trio(raw.at[0], t)
            moved = apply(centre, neighbours(centre, above, below), w)
            g_ref[at(t), :] = 0.25 * (moved - centre) + raw[4, at(t), :]
            return carry

        lax.fori_loop(lo, hi, body, 0)

    prepare(first + 1, last - 1)

    for side in range(2):
        edge = (0, pad + rows)[side]

        @pl.when(has[side])
        def _():
            remote(side, side).wait_recv()
            for a in range(5):
                raw[a, pl.ds(edge, pad), :] = recv[side, a].astype(jnp.float32)

        @pl.when(jnp.logical_not(has[side]))
        def _():
            for a in range(5):
                raw[a, pl.ds(edge, pad), :] = jnp.zeros((pad, cols), jnp.float32)

    low = (pad - halo + 1) // TILE
    high = -((-(pad + rows + halo - 1)) // TILE)
    prepare(low, first + 1)
    prepare(last - 1, high)

    def coefficient(j):
        value = jnp.float32(table[0][j])
        for n in range(1, len(table)):
            value = jnp.where(turn == n, jnp.float32(table[n][j]), value)
        return value

    def step(source, scale, target, q, lo, hi):
        def body(t, carry):
            centre, above, below = trio(source, t)
            around = neighbours(centre, above, below)
            w = [wts[j, at(t), :] for j in range(5)]
            value = apply(centre, around, w)
            if scale is not None:
                value = scale * value
            value = value + q * g_ref[at(t), :]
            if target is None:
                here = pl.ds(pl.multiple_of((t - first) * TILE, TILE), TILE)
                out_ref[0, here, :] = raw[0, at(t), :] + value
            else:
                target[at(t), :] = value
            return carry

        lax.fori_loop(lo, hi, body, 0)

    for m in range(degree):
        reach = degree - 1 - m
        lo = (pad - reach) // TILE
        hi = -((-(pad + rows + reach)) // TILE)
        source = g_ref if m == 0 else y_ref.at[(m - 1) % 2]
        scale = coefficient(degree) if m == 0 else None
        target = None if m == degree - 1 else y_ref.at[m % 2]
        step(source, scale, target, coefficient(degree - 1 - m), lo, hi)

    for side in range(2):
        @pl.when(has[side])
        def _():
            remote(side, 1 - side).wait_send()


def per_device(table, blocks, *args):
    rows, cols = args[0].shape
    halo = len(table[0])
    pad = -(-halo // 16) * 16
    ext = rows + 2 * pad
    f32, bf16 = jnp.float32, jnp.bfloat16
    return pl.pallas_call(
        functools.partial(kernel, table, halo, pad, blocks),
        out_shape=jax.ShapeDtypeStruct((1, rows, cols), f32),
        in_specs=[pl.BlockSpec(memory_space=pl.ANY)] * 5,
        out_specs=pl.BlockSpec(memory_space=pltpu.VMEM),
        scratch_shapes=[
            pltpu.VMEM((5, ext, cols), f32),
            pltpu.VMEM((5, ext, cols), f32),
            pltpu.VMEM((ext, cols), f32),
            pltpu.VMEM((2, ext, cols), f32),
            pltpu.VMEM((2, 5, pad, cols), bf16),
            pltpu.VMEM((2, 5, pad, cols), bf16),
            pltpu.SemaphoreType.DMA((5,)),
            pltpu.SemaphoreType.DMA((2,)),
            pltpu.SemaphoreType.DMA((2,)),
        ],
        compiler_params=pltpu.CompilerParams(
            collective_id=0, has_side_effects=True, vmem_limit_bytes=48 * 1024 * 1024
        ),
    )(*args)


def solution(mesh):
    table = end_polynomials(mesh.shape["tm"])
    spec = P(("ens", "space"), None)
    return jax.shard_map(
        functools.partial(per_device, table, mesh.shape["space"]),
        mesh=mesh,
        in_specs=(spec,) * 5,
        out_specs=P("tm", ("ens", "space"), None),
        check_vma=False,
    )
```

```python
import functools
from fractions import Fraction

import jax
import jax.numpy as jnp
from jax import lax
from jax.experimental import pallas as pl
from jax.experimental.pallas import tpu as pltpu
from jax.sharding import PartitionSpec as P

FINE = 4
TILE = 8
UNROLL = 4
STRAIGHT = 3
MESH = pl.DeviceIdType.MESH


def poly_add(a, b, sign=1):
    size = max(len(a), len(b))
    a, b = (list(x) + [Fraction(0)] * (size - len(x)) for x in (a, b))
    return [x + sign * y for x, y in zip(a, b)]


def poly_mul(a, b):
    out = [Fraction(0)] * (len(a) + len(b) - 1)
    for i, x in enumerate(a):
        for j, y in enumerate(b):
            out[i + j] += x * y
    return out


def end_polynomials(slices):
    fine_step = [Fraction(FINE - 1, FINE), Fraction(1, FINE)]
    power, total = [Fraction(1)], [Fraction(0)]
    for _ in range(FINE):
        total = poly_add(total, power)
        power = poly_mul(power, fine_step)

    def fine(q):
        return poly_add(poly_mul(power, q), total)

    def coarse(q):
        return poly_add([Fraction(0)] + list(q), [Fraction(FINE)])

    start_one = start_two = [Fraction(0)]
    delta_zero = poly_add(fine(start_one), coarse(start_one), -1)
    ends = []
    for _ in range(slices):
        delta_one = poly_add(fine(start_one), coarse(start_one), -1)
        start_two = poly_add(coarse(start_two), delta_one)
        ends.append(list(start_two))
        start_one = poly_add(coarse(start_one), delta_zero)
    for q in ends:
        while len(q) > 1 and q[-1] == 0:
            q.pop()
    degree = max(len(q) for q in ends) - 1
    return [[float(c) for c in q] + [0.0] * (degree + 1 - len(q)) for q in ends]


def neighbours(centre, above, below):
    rows, cols = centre.shape
    sub = lax.broadcasted_iota(jnp.int32, (rows, cols), 0)
    east = pltpu.roll(centre, cols - 1, 1)
    west = pltpu.roll(centre, 1, 1)
    north = pltpu.roll(jnp.where(sub == rows - 1, above, centre), 1, 0)
    south = pltpu.roll(jnp.where(sub == 0, below, centre), rows - 1, 0)
    return east, west, north, south


def over(lo, hi, body):
    size = hi - lo
    if size <= STRAIGHT:
        for t in range(lo, hi):
            body(t)
        return
    def several(i, carry):
        for j in range(UNROLL):
            body(lo + i * UNROLL + j)
        return carry

    lax.fori_loop(0, size // UNROLL, several, 0)
    for t in range(hi - size % UNROLL, hi):
        body(t)


def kernel(table, halo, pad, blocks, overlap, *refs):
    args, out_ref = refs[:5], refs[5]
    raw, wts, g_ref, y_ref, send, recv, in_sem, send_sem, recv_sem = refs[6:]
    rows, cols = args[0].shape
    tiles = (rows + 2 * pad) // TILE
    first, last = pad // TILE, (pad + rows) // TILE
    degree = len(table[0]) - 1
    me, turn = lax.axis_index("space"), lax.axis_index("tm")
    has = (me > 0, me < blocks - 1)
    peer = (me - 1, me + 1)

    loads = [
        pltpu.make_async_copy(args[a], raw.at[a, pl.ds(pad, rows)], in_sem.at[a])
        for a in range(5)
    ]
    for load in loads:
        load.start()
    barrier = pltpu.get_barrier_semaphore()
    for side in range(2):
        @pl.when(has[side])
        def _():
            pl.semaphore_signal(
                barrier, inc=1, device_id={"space": peer[side]}, device_id_type=MESH
            )

    def remote(side, slot):
        return pltpu.make_async_remote_copy(
            src_ref=send.at[side],
            dst_ref=recv.at[slot],
            send_sem=send_sem.at[side],
            recv_sem=recv_sem.at[slot],
            device_id={"space": peer[side]},
            device_id_type=MESH,
        )

    for a in range(5):
        loads[a].wait()
        send[0, a] = raw[a, pl.ds(pad, pad), :].astype(jnp.bfloat16)
        send[1, a] = raw[a, pl.ds(rows, pad), :].astype(jnp.bfloat16)
    peers = has[0].astype(jnp.int32) + has[1].astype(jnp.int32)
    pl.semaphore_wait(barrier, peers)
    for side in range(2):
        @pl.when(has[side])
        def _():
            remote(side, 1 - side).start()

    def at(t):
        return pl.ds(t * TILE if isinstance(t, int) else pl.multiple_of(t * TILE, TILE), TILE)

    def trio(ref, t):
        return (
            ref[at(t), :],
            ref[at(max(t - 1, 0) if isinstance(t, int) else jnp.maximum(t - 1, 0)), :],
            ref[at(min(t + 1, tiles - 1) if isinstance(t, int) else jnp.minimum(t + 1, tiles - 1)), :],
        )

    def apply(centre, around, w):
        east, west, north, south = around
        return (w[0] * east + w[1] * west) + (w[2] * north + w[3] * south) + w[4] * centre

    def prepare(lo, hi):
        def body(t):
            k = 4.0 * raw[1, at(t), :]
            p, r = 2.0 * raw[2, at(t), :], 2.0 * raw[3, at(t), :]
            w = (k - p, k + p, k + r, k - r, 1.0 - 4.0 * k)
            for j in range(5):
                wts[j, at(t), :] = w[j]
            centre, above, below = trio(raw.at[0], t)
            moved = apply(centre, neighbours(centre, above, below), w)
            g_ref[at(t), :] = 0.25 * (moved - centre) + raw[4, at(t), :]

        over(lo, hi, body)

    def step(source, scale, target, q, lo, hi):
        def body(t):
            centre, above, below = trio(source, t)
            around = neighbours(centre, above, below)
            w = [wts[j, at(t), :] for j in range(5)]
            value = apply(centre, around, w)
            if scale is not None:
                value = scale * value
            value = value + q * g_ref[at(t), :]
            if target is None:
                here = at(t - first)
                out_ref[0, here, :] = raw[0, at(t), :] + value
            else:
                target[at(t), :] = value

        over(lo, hi, body)

    def coefficient(j):
        value = jnp.float32(table[0][j])
        for n in range(1, len(table)):
            value = jnp.where(turn == n, jnp.float32(table[n][j]), value)
        return value

    def advance(m, spans):
        slots = y_ref.shape[0]
        source = g_ref if m == 0 else y_ref.at[(m - 1) % slots]
        scale = coefficient(degree) if m == 0 else None
        target = None if m == degree - 1 else y_ref.at[m % slots]
        q = coefficient(degree - 1 - m)
        for lo, hi in spans:
            step(source, scale, target, q, lo, hi)

    prepare(first, last)
    if overlap:
        for m in range(degree):
            advance(m, [(first, last)])

    for side in range(2):
        edge = (0, pad + rows)[side]

        @pl.when(has[side])
        def _():
            remote(side, side).wait_recv()
            for a in range(5):
                raw[a, pl.ds(edge, pad), :] = recv[side, a].astype(jnp.float32)

        @pl.when(jnp.logical_not(has[side]))
        def _():
            for a in range(5):
                raw[a, pl.ds(edge, pad), :] = jnp.zeros((pad, cols), jnp.float32)

    low = (pad - halo + 1) // TILE
    high = -((-(pad + rows + halo - 1)) // TILE)
    prepare(low, first + 1)
    prepare(last - 1, high)

    for m in range(degree):
        reach = degree - 1 - m
        lo = (pad - reach) // TILE
        hi = -((-(pad + rows + reach)) // TILE)
        if overlap:
            inner = -(-(pad + m + 2) // TILE)
            advance(m, [(lo, inner), (first + last - inner, hi)])
        else:
            advance(m, [(lo, hi)])

    for side in range(2):
        @pl.when(has[side])
        def _():
            remote(side, 1 - side).wait_send()


def per_device(table, blocks, *args):
    rows, cols = args[0].shape
    halo = len(table[0])
    pad = -(-halo // 16) * 16
    ext = rows + 2 * pad
    overlap = halo <= 12 and rows >= 4 * TILE
    f32, bf16 = jnp.float32, jnp.bfloat16
    return pl.pallas_call(
        functools.partial(kernel, table, halo, pad, blocks, overlap),
        out_shape=jax.ShapeDtypeStruct((1, rows, cols), f32),
        in_specs=[pl.BlockSpec(memory_space=pl.ANY)] * 5,
        out_specs=pl.BlockSpec(memory_space=pltpu.VMEM),
        scratch_shapes=[
            pltpu.VMEM((5, ext, cols), f32),
            pltpu.VMEM((5, ext, cols), f32),
            pltpu.VMEM((ext, cols), f32),
            pltpu.VMEM((halo - 2 if overlap else 2, ext, cols), f32),
            pltpu.VMEM((2, 5, pad, cols), bf16),
            pltpu.VMEM((2, 5, pad, cols), bf16),
            pltpu.SemaphoreType.DMA((5,)),
            pltpu.SemaphoreType.DMA((2,)),
            pltpu.SemaphoreType.DMA((2,)),
        ],
        compiler_params=pltpu.CompilerParams(
            collective_id=0, has_side_effects=True, vmem_limit_bytes=63 * 1024 * 1024
        ),
    )(*args)


def solution(mesh):
    table = end_polynomials(mesh.shape["tm"])
    spec = P(("ens", "space"), None)
    return jax.shard_map(
        functools.partial(per_device, table, mesh.shape["space"]),
        mesh=mesh,
        in_specs=(spec,) * 5,
        out_specs=P("tm", ("ens", "space"), None),
        check_vma=False,
    )
```

```python
import functools
from fractions import Fraction

import jax
import jax.numpy as jnp
from jax import lax
from jax.experimental import pallas as pl
from jax.experimental.pallas import tpu as pltpu
from jax.sharding import PartitionSpec as P

FINE = 4
TILE = 8
UNROLL = 8
STRAIGHT = 8
MESH = pl.DeviceIdType.MESH


def poly_add(a, b, sign=1):
    size = max(len(a), len(b))
    a, b = (list(x) + [Fraction(0)] * (size - len(x)) for x in (a, b))
    return [x + sign * y for x, y in zip(a, b)]


def poly_mul(a, b):
    out = [Fraction(0)] * (len(a) + len(b) - 1)
    for i, x in enumerate(a):
        for j, y in enumerate(b):
            out[i + j] += x * y
    return out


def end_polynomials(slices):
    fine_step = [Fraction(FINE - 1, FINE), Fraction(1, FINE)]
    power, total = [Fraction(1)], [Fraction(0)]
    for _ in range(FINE):
        total = poly_add(total, power)
        power = poly_mul(power, fine_step)

    def fine(q):
        return poly_add(poly_mul(power, q), total)

    def coarse(q):
        return poly_add([Fraction(0)] + list(q), [Fraction(FINE)])

    start_one = start_two = [Fraction(0)]
    delta_zero = poly_add(fine(start_one), coarse(start_one), -1)
    ends = []
    for _ in range(slices):
        delta_one = poly_add(fine(start_one), coarse(start_one), -1)
        start_two = poly_add(coarse(start_two), delta_one)
        ends.append(list(start_two))
        start_one = poly_add(coarse(start_one), delta_zero)
    for q in ends:
        while len(q) > 1 and q[-1] == 0:
            q.pop()
    degree = max(len(q) for q in ends) - 1
    return [[float(c) for c in q] + [0.0] * (degree + 1 - len(q)) for q in ends]


def neighbours(centre, above, below):
    rows, cols = centre.shape
    sub = lax.broadcasted_iota(jnp.int32, (rows, cols), 0)
    east = pltpu.roll(centre, cols - 1, 1)
    west = pltpu.roll(centre, 1, 1)
    north = pltpu.roll(jnp.where(sub == rows - 1, above, centre), 1, 0)
    south = pltpu.roll(jnp.where(sub == 0, below, centre), rows - 1, 0)
    return east, west, north, south


def over(lo, hi, body):
    size = hi - lo
    if size <= STRAIGHT:
        for t in range(lo, hi):
            body(t)
        return
    def several(i, carry):
        for j in range(UNROLL):
            body(lo + i * UNROLL + j)
        return carry

    lax.fori_loop(0, size // UNROLL, several, 0)
    for t in range(hi - size % UNROLL, hi):
        body(t)


def kernel(table, halo, pad, blocks, overlap, *refs):
    args, out_ref = refs[:5], refs[5]
    raw, wts, g_ref, y_ref, pack, send, recv, in_sem, send_sem, recv_sem = refs[6:]
    rows, cols = args[0].shape
    tiles = (rows + 2 * pad) // TILE
    first, last = pad // TILE, (pad + rows) // TILE
    degree = len(table[0]) - 1
    me, turn = lax.axis_index("space"), lax.axis_index("tm")
    has = (me > 0, me < blocks - 1)
    peer = (me - 1, me + 1)

    pieces = ((0, pad), (rows - pad, pad), (pad, rows - 2 * pad))
    loads = [
        [
            pltpu.make_async_copy(
                args[a].at[pl.ds(r, size)], raw.at[a, pl.ds(pad + r, size)], in_sem.at[a, piece]
            )
            for a in range(5)
        ]
        for piece, (r, size) in enumerate(pieces)
        if size > 0
    ]
    for piece in loads:
        for load in piece:
            load.start()
    barrier = pltpu.get_barrier_semaphore()
    for side in range(2):
        @pl.when(has[side])
        def _():
            pl.semaphore_signal(
                barrier, inc=1, device_id={"space": peer[side]}, device_id_type=MESH
            )

    def remote(side, slot):
        return pltpu.make_async_remote_copy(
            src_ref=send.at[side],
            dst_ref=recv.at[slot],
            send_sem=send_sem.at[side],
            recv_sem=recv_sem.at[slot],
            device_id={"space": peer[side]},
            device_id_type=MESH,
        )

    near = halo // TILE * TILE
    far = [(0, 5 * near, halo - near)]
    for a in range(1, 5):
        far.append((a, far[-1][1] + far[-1][2], max(halo - near - 1, 0)))
    far = [entry for entry in far if entry[2] > 0]
    spare = send.shape[1] - 5 * near
    if spare > 0:
        for side in range(2):
            pack[side, pl.ds(5 * near, spare), :] = jnp.zeros((spare, cols), jnp.float32)
    for a in range(5):
        loads[0][a].wait()
        loads[1][a].wait()
        pack[0, pl.ds(a * near, near), :] = raw[a, pl.ds(pad, near), :]
        pack[1, pl.ds(a * near, near), :] = raw[a, pl.ds(pad + rows - near, near), :]
    for a, place, count in far:
        pack[0, pl.ds(place, count), :] = raw[a, pl.ds(pad + near, count), :]
        pack[1, pl.ds(place, count), :] = raw[a, pl.ds(pad + rows - near - count, count), :]
    send[...] = pack[...].astype(jnp.bfloat16)
    peers = has[0].astype(jnp.int32) + has[1].astype(jnp.int32)
    pl.semaphore_wait(barrier, peers)
    for side in range(2):
        @pl.when(has[side])
        def _():
            remote(side, 1 - side).start()

    def at(t):
        return pl.ds(t * TILE if isinstance(t, int) else pl.multiple_of(t * TILE, TILE), TILE)

    def trio(ref, t):
        return (
            ref[at(t), :],
            ref[at(max(t - 1, 0) if isinstance(t, int) else jnp.maximum(t - 1, 0)), :],
            ref[at(min(t + 1, tiles - 1) if isinstance(t, int) else jnp.minimum(t + 1, tiles - 1)), :],
        )

    def apply(centre, around, w):
        east, west, north, south = around
        return (w[0] * east + w[1] * west) + (w[2] * north + w[3] * south) + w[4] * centre

    def prepare(lo, hi):
        def body(t):
            k = 4.0 * raw[1, at(t), :]
            p, r = 2.0 * raw[2, at(t), :], 2.0 * raw[3, at(t), :]
            w = (k - p, k + p, k + r, k - r, 1.0 - 4.0 * k)
            for j in range(5):
                wts[j, at(t), :] = w[j]
            centre, above, below = trio(raw.at[0], t)
            moved = apply(centre, neighbours(centre, above, below), w)
            g_ref[at(t), :] = 0.25 * (moved - centre) + raw[4, at(t), :]

        over(lo, hi, body)

    def step(source, scale, target, q, lo, hi):
        def body(t):
            centre, above, below = trio(source, t)
            around = neighbours(centre, above, below)
            w = [wts[j, at(t), :] for j in range(5)]
            value = apply(centre, around, w)
            if scale is not None:
                value = scale * value
            value = value + q * g_ref[at(t), :]
            if target is None:
                here = at(t - first)
                out_ref[0, here, :] = raw[0, at(t), :] + value
            else:
                target[at(t), :] = value

        over(lo, hi, body)

    def coefficient(j):
        value = jnp.float32(table[0][j])
        for n in range(1, len(table)):
            value = jnp.where(turn == n, jnp.float32(table[n][j]), value)
        return value

    def advance(m, spans):
        slots = y_ref.shape[0]
        source = g_ref if m == 0 else y_ref.at[(m - 1) % slots]
        scale = coefficient(degree) if m == 0 else None
        target = None if m == degree - 1 else y_ref.at[m % slots]
        q = coefficient(degree - 1 - m)
        for lo, hi in spans:
            step(source, scale, target, q, lo, hi)

    for piece in loads[2:]:
        for load in piece:
            load.wait()

    prepare(first, last)
    if overlap:
        redone = -(-(degree + 1) // TILE)
        for m in range(degree):
            skip = max(0, redone - (degree - 1 - m))
            advance(m, [(first + skip, last - skip)])

    for side in range(2):
        edge = (0, pad + rows)[side]

        @pl.when(has[side])
        def _():
            remote(side, side).wait_recv()
            pack[side] = recv[side].astype(jnp.float32)
            beside = (pad - near, pad + rows)[side]
            for a in range(5):
                raw[a, pl.ds(beside, near), :] = pack[side, pl.ds(a * near, near), :]
            for a, place, count in far:
                away = (pad - near - count, pad + rows + near)[side]
                raw[a, pl.ds(away, count), :] = pack[side, pl.ds(place, count), :]

        @pl.when(jnp.logical_not(has[side]))
        def _():
            for a in range(5):
                raw[a, pl.ds(edge, pad), :] = jnp.zeros((pad, cols), jnp.float32)

    low = (pad - halo + 1) // TILE
    high = -((-(pad + rows + halo - 1)) // TILE)
    prepare(low, first + 1)
    prepare(last - 1, high)

    for m in range(degree):
        reach = degree - 1 - m
        lo = (pad - reach) // TILE
        hi = -((-(pad + rows + reach)) // TILE)
        if overlap:
            inner = -(-(pad + m + 2) // TILE)
            advance(m, [(lo, inner), (first + last - inner, hi)])
        else:
            advance(m, [(lo, hi)])

    for side in range(2):
        @pl.when(has[side])
        def _():
            remote(side, 1 - side).wait_send()


def per_device(table, blocks, *args):
    rows, cols = args[0].shape
    halo = len(table[0])
    pad = -(-halo // 16) * 16
    ext = rows + 2 * pad
    overlap = halo <= 12 and rows >= 4 * TILE
    far = halo % TILE
    packed = -(-(5 * (halo - far) + 5 * far - min(far, 1) * 4) // 16) * 16
    f32, bf16 = jnp.float32, jnp.bfloat16
    return pl.pallas_call(
        functools.partial(kernel, table, halo, pad, blocks, overlap),
        out_shape=jax.ShapeDtypeStruct((1, rows, cols), f32),
        in_specs=[pl.BlockSpec(memory_space=pl.ANY)] * 5,
        out_specs=pl.BlockSpec(memory_space=pltpu.VMEM),
        scratch_shapes=[
            pltpu.VMEM((5, ext, cols), f32),
            pltpu.VMEM((5, ext, cols), f32),
            pltpu.VMEM((ext, cols), f32),
            pltpu.VMEM((halo - 2 if overlap else 2, ext, cols), f32),
            pltpu.VMEM((2, packed, cols), f32),
            pltpu.VMEM((2, packed, cols), bf16),
            pltpu.VMEM((2, packed, cols), bf16),
            pltpu.SemaphoreType.DMA((5, 3)),
            pltpu.SemaphoreType.DMA((2,)),
            pltpu.SemaphoreType.DMA((2,)),
        ],
        compiler_params=pltpu.CompilerParams(
            collective_id=0, has_side_effects=True, vmem_limit_bytes=63 * 1024 * 1024
        ),
    )(*args)


def solution(mesh):
    table = end_polynomials(mesh.shape["tm"])
    spec = P(("ens", "space"), None)
    return jax.shard_map(
        functools.partial(per_device, table, mesh.shape["space"]),
        mesh=mesh,
        in_specs=(spec,) * 5,
        out_specs=P("tm", ("ens", "space"), None),
        check_vma=False,
    )
```
